256 devices in a mesh: row: 8 (over x, y_lo), col: 32 (over z, y_hi, core).
Axes of the slice: x: 4, y: 4 (y_hi: 2, y_lo: 2; y = y_hi * 2 + y_lo), z: 8, core: 2. Of those that a mesh axis runs over, the one named last changes fastest.
Arguments:
- queries: bfloat16 [1024, 2560], P(('row', 'col')), may hold values from -4 to 4
- passages: bfloat16 [1024, 2560], P(('row', 'col')), may hold values from -1 to 1
- positive: int32 [1024], P(('row', 'col')), may hold values from 0 to 1023, each once
Outputs:
- loss: float32 [], replicated
- grad_queries: bfloat16 [1024, 2560], P(('row', 'col'))
- grad_passages: bfloat16 [1024, 2560], P(('row', 'col'))
The draws below stay inside these ranges and needn't reach their ends.
Inputs may be any that keep to these rules, and one draw needn't show every extreme that they name: Each passage is the positive of exactly one query.
All inputs are finite; a program needn't handle non-finite values.
Results may differ from the reference program's by a relative error of at most 0.0045.
Values may be sent and summed in bfloat16 or wider, within the bound.
A program may use at most 64 MiB of HBM per device.

```python
import math
import jax
import jax.numpy as jnp
from jax import lax

D = 2560
N = 1024


def shared_rows(key):
    return 0.2 * jax.random.truncated_normal(jax.random.fold_in(key, 100), -4.0, 4.0, (N, D), jnp.float32)


def draw_passages(key, part):
    shared = shared_rows(key)
    return shared.astype(jnp.bfloat16)


def draw_queries(key, part):
    key = jax.random.fold_in(key, 23)
    return (0.2 * jax.random.truncated_normal(key, -4.0, 4.0, (N, D), jnp.float32)).astype(jnp.bfloat16)


def setup_inputs(seed: int = 0) -> dict:
    key_list = jax.random.split(jax.random.key(seed), 4)
    queries = draw_queries(jax.random.fold_in(key_list[3], 71), 0)
    passages = draw_passages(jax.random.fold_in(key_list[3], 71), 0)
    positive = jax.random.permutation(key_list[2], N).astype(jnp.int32)
    return dict(queries=queries, passages=passages, positive=positive)


def reference(queries, passages, positive):
    total = queries.shape[0]
    height = math.gcd(total, 512)
    count_blocks = total // height
    query_blocks = queries.reshape(count_blocks, height, queries.shape[1])
    target_blocks = positive.reshape(count_blocks, height)
    columns = jnp.arange(total, dtype=jnp.int32)

    def step(carry, inputs):
        grad_pass, loss_sum = carry
        query_block, target_block = inputs
        scores = lax.dot_general(query_block, passages, (((1,), (1,)), ((), ())), preferred_element_type=jnp.float32)
        row_peak = jnp.max(scores, axis=1)
        powers = jnp.exp(scores - row_peak[:, None])
        totals = jnp.sum(powers, axis=1)
        matched = target_block.astype(jnp.int32)[:, None] == columns[None, :]
        positive_score = jnp.sum(jnp.where(matched, scores, jnp.zeros_like(scores)), axis=1)
        loss_sum = loss_sum + jnp.sum(row_peak + jnp.log(totals) - positive_score)
        weights = (powers / totals[:, None] - matched.astype(jnp.float32)).astype(jnp.bfloat16)
        grad_query = jnp.dot(weights, passages, preferred_element_type=jnp.float32).astype(jnp.bfloat16)
        grad_pass = grad_pass + lax.dot_general(weights, query_block, (((0,), (0,)), ((), ())), preferred_element_type=jnp.float32)
        return (grad_pass, loss_sum), grad_query

    init = (jnp.zeros(passages.shape, jnp.float32), jnp.zeros((), jnp.float32))
    (grad_pass, loss_sum), grad_queries = lax.scan(step, init, (query_blocks, target_blocks))
    return loss_sum / total, grad_queries.reshape(queries.shape), grad_pass.astype(jnp.bfloat16)
```

```python
import functools

import jax
import jax.numpy as jnp
from jax import lax
from jax.experimental import pallas as pl
from jax.experimental.pallas import tpu as pltpu
from jax.sharding import PartitionSpec as P

MESH = pl.DeviceIdType.MESH
X, Y, Z, CORES = 4, 4, 8, 2
PLANE = X * Y
LANES = 128
F32, BF16 = jnp.float32, jnp.bfloat16


def device_of(x, y, z, core):
    return (x * 2 + y % 2, z * 4 + (y // 2) * 2 + core)


def kernel(total, q_ref, p_ref, pos_ref, loss_ref, gq_ref, gp_ref,
           stage, qbuf, pbuf, qwide, pwide, half_own, half_other, statbuf, stat_own,
           gq_send, gq_recv, gp_send, gp_recv, lossbuf, loss_own,
           local_sem, send_sem, recv_sem):
    row, col = lax.axis_index("row"), lax.axis_index("col")
    x, z, core = row // 2, col // 4, col % 2
    y = ((col // 2) % 2) * 2 + row % 2
    chip = x * Y + y
    own = q_ref.shape[0]
    half = q_ref.shape[1] // CORES
    q_slot, p_slot = chip * CORES + core, z * CORES + core
    other = device_of(x, y, z, 1 - core)

    def plane_peer(step):
        to = (chip + step) % PLANE
        return to, to // Y, to % Y

    barrier = pltpu.get_barrier_semaphore()

    def greet_plane(step, _):
        _, px, py = plane_peer(step)
        for c in range(CORES):
            pl.semaphore_signal(barrier, inc=1, device_id=device_of(px, py, z, c), device_id_type=MESH)
        return _

    def greet_line(step, _):
        for c in range(CORES):
            pl.semaphore_signal(barrier, inc=1, device_id=device_of(x, y, (z + step) % Z, c), device_id_type=MESH)
        return _

    pl.semaphore_signal(barrier, inc=1, device_id=other, device_id_type=MESH)
    lax.fori_loop(1, PLANE, greet_plane, 0)
    lax.fori_loop(1, Z, greet_line, 0)

    lane = lax.broadcasted_iota(jnp.int32, (1, LANES), 1)
    for h in range(CORES):
        stage[h, :, :half] = q_ref[:, h * half:(h + 1) * half]
    codes = []
    for k in range(own):
        index = pos_ref[k]
        codes.append(((lane == index // 32) | (lane == 32 + index % 32)).astype(F32))
    code = jnp.concatenate(codes, axis=0).astype(BF16)
    for h in range(CORES):
        stage[h, :, half:] = code

    pl.semaphore_wait(barrier, PLANE * CORES + (Z - 1) * CORES - 1)

    def send(src, dst, to, kind):
        return pltpu.make_async_remote_copy(
            src_ref=src, dst_ref=dst, send_sem=send_sem.at[kind], recv_sem=recv_sem.at[kind],
            device_id=to, device_id_type=MESH)

    def p_half(h):
        return p_ref.at[:, pl.ds(pl.multiple_of(h * half, LANES), half)]

    def gather_plane(step, _):
        _, px, py = plane_peer(step)
        for c in range(CORES):
            send(stage.at[c], qbuf.at[q_slot], device_of(px, py, z, c), 0).start()
        return _

    def gather_line(step, _):
        for c in range(CORES):
            send(p_half(c), pbuf.at[p_slot], device_of(x, y, (z + step) % Z, c), 1).start()
        return _

    lax.fori_loop(1, Z, gather_line, 0)
    lax.fori_loop(1, PLANE, gather_plane, 0)
    send(stage.at[1 - core], qbuf.at[q_slot], other, 0).start()
    send(p_half(1 - core), pbuf.at[p_slot], other, 1).start()
    own_q = pltpu.make_async_copy(stage.at[core], qbuf.at[q_slot], local_sem.at[0])
    own_p = pltpu.make_async_copy(p_half(core), pbuf.at[p_slot], local_sem.at[1])
    own_q.start()
    own_p.start()
    own_q.wait()
    own_p.wait()

    def wait_recv(ref, kind):
        pltpu.make_async_copy(ref, ref, recv_sem.at[kind]).wait()

    def wait_send(ref, kind):
        pltpu.make_async_copy(ref, ref, send_sem.at[kind]).wait()

    p_count, q_count = Z * CORES, PLANE * CORES
    wait_recv(pbuf.at[pl.ds(0, p_count - 1)], 1)
    for s in range(p_count):
        pwide[s * own:(s + 1) * own, :] = pbuf[s].astype(F32)
    passages = pwide[...].astype(BF16)
    wait_recv(qbuf.at[pl.ds(0, q_count - 1)], 0)
    for s in range(q_count):
        qwide[s * own:(s + 1) * own, :] = qbuf[s].astype(F32)
    queries = qwide[:, :half].astype(BF16)
    q_code = qwide[:, half:].astype(BF16)

    contract_last = (((1,), (1,)), ((), ()))
    half_own[...] = lax.dot_general(passages, queries, contract_last, preferred_element_type=F32)
    trade = send(half_own, half_other, other, 2)
    trade.start()
    n_p = p_count * own
    slot = lax.broadcasted_iota(jnp.int32, (n_p, LANES), 0)
    zz, cc, kk = slot // (CORES * own), (slot // own) % CORES, slot % own
    p_row, p_col = device_of(x, y, zz, cc)
    p_id = (p_row * 32 + p_col) * own + kk
    p_lane = lax.broadcasted_iota(jnp.int32, (n_p, LANES), 1)
    p_code = ((p_lane == p_id // 32) | (p_lane == 32 + p_id % 32)).astype(F32).astype(BF16)
    matched = lax.dot_general(p_code, q_code, contract_last, preferred_element_type=F32) > 1.5
    trade.wait()
    scores = half_own[...] + half_other[...]

    peak = jnp.max(scores, axis=0, keepdims=True)
    summed = jnp.sum(jnp.exp(scores - peak), axis=0, keepdims=True)
    picked = jnp.sum(jnp.where(matched, scores, 0.0), axis=0, keepdims=True)
    stat_own[0:1, :] = peak
    stat_own[1:2, :] = summed
    stat_own[2:3, :] = picked
    stat_own[3:8, :] = jnp.zeros((5, stat_own.shape[1]), F32)
    statbuf[pl.ds(chip, 1)] = stat_own[...][None]

    def send_stat(step, _):
        _, px, py = plane_peer(step)
        send(stat_own, statbuf.at[chip], device_of(px, py, z, core), 3).start()
        return _

    lax.fori_loop(1, PLANE, send_stat, 0)
    wait_recv(statbuf.at[pl.ds(0, PLANE - 1)], 3)
    stats = statbuf[...]
    peaks, sums, picks = stats[:, 0:1], stats[:, 1:2], stats[:, 2:3]
    row_peak = jnp.max(peaks, axis=0)
    totals = jnp.sum(sums * jnp.exp(peaks - row_peak[None]), axis=0)
    positive_score = jnp.sum(picks, axis=0)
    weights = (jnp.exp(scores - row_peak) / totals - matched.astype(F32)).astype(BF16)

    for at in range(0, half, 256):
        part = lax.dot_general(weights, passages[:, at:at + 256], (((0,), (0,)), ((), ())),
                               preferred_element_type=F32).astype(BF16)
        for s in range(q_count):
            gq_send[s, :, at:at + 256] = part[s * own:(s + 1) * own]

    def give_plane(step, _):
        to, px, py = plane_peer(step)
        for c in range(CORES):
            send(gq_send.at[to * CORES + c], gq_recv.at[chip, core], device_of(px, py, z, c), 4).start()
        return _

    lax.fori_loop(1, PLANE, give_plane, 0)
    send(gq_send.at[chip * CORES + 1 - core], gq_recv.at[chip, core], other, 4).start()
    own_gq = pltpu.make_async_copy(gq_send.at[q_slot], gq_recv.at[chip, core], local_sem.at[2])
    own_gq.start()
    for at in range(0, half, 256):
        part = jnp.dot(weights, queries[:, at:at + 256], preferred_element_type=F32).astype(BF16)
        for s in range(p_count):
            gp_send[s, :, at:at + 256] = part[s * own:(s + 1) * own]

    def give_line(step, _):
        to = (z + step) % Z
        for c in range(CORES):
            send(gp_send.at[to * CORES + c], gp_recv.at[z, core], device_of(x, y, to, c), 5).start()
        return _

    lax.fori_loop(1, Z, give_line, 0)
    send(gp_send.at[z * CORES + 1 - core], gp_recv.at[z, core], other, 5).start()
    own_gp = pltpu.make_async_copy(gp_send.at[p_slot], gp_recv.at[z, core], local_sem.at[3])
    own_gp.start()

    block_loss = row_peak + jnp.log(totals) - positive_score
    loss_own[...] = jnp.broadcast_to(block_loss, loss_own.shape)
    lossbuf[pl.ds(z, 1)] = loss_own[...][None]

    def give_loss(step, _):
        send(loss_own, lossbuf.at[z], device_of(x, y, (z + step) % Z, core), 6).start()
        return _

    lax.fori_loop(1, Z, give_loss, 0)
    wait_recv(lossbuf.at[pl.ds(0, Z - 1)], 6)
    loss_ref[0, 0] = jnp.sum(jnp.sum(lossbuf[...], axis=0)[0:1]) / total

    own_gp.wait()
    wait_recv(gp_send.at[pl.ds(0, p_count - 1)], 5)
    for h in range(CORES):
        acc = gp_recv[0, h].astype(F32)
        for k in range(1, Z):
            acc += gp_recv[k, h].astype(F32)
        gp_ref[:, h * half:(h + 1) * half] = acc.astype(BF16)
    own_gq.wait()
    wait_recv(gq_send.at[pl.ds(0, q_count - 1)], 4)
    for h in range(CORES):
        acc = gq_recv[0, h].astype(F32)
        for k in range(1, PLANE):
            acc += gq_recv[k, h].astype(F32)
        gq_ref[:, h * half:(h + 1) * half] = acc.astype(BF16)

    wait_send(qbuf.at[pl.ds(0, q_count - 1)], 0)
    wait_send(pbuf.at[pl.ds(0, p_count - 1)], 1)
    wait_send(statbuf.at[pl.ds(0, PLANE - 1)], 3)
    wait_send(gq_send.at[pl.ds(0, q_count - 1)], 4)
    wait_send(gp_send.at[pl.ds(0, p_count - 1)], 5)
    wait_send(lossbuf.at[pl.ds(0, Z - 1)], 6)


def per_device(queries, passages, positive):
    own, width = queries.shape
    half = width // CORES
    n_q, n_p = PLANE * CORES, Z * CORES
    vmem = pl.BlockSpec(memory_space=pltpu.VMEM)
    loss, gq, gp = pl.pallas_call(
        functools.partial(kernel, n_q * own * Z),
        out_shape=(
            jax.ShapeDtypeStruct((1, 1), F32),
            jax.ShapeDtypeStruct((own, width), BF16),
            jax.ShapeDtypeStruct((own, width), BF16),
        ),
        in_specs=[vmem, vmem, pl.BlockSpec(memory_space=pltpu.SMEM)],
        out_specs=(pl.BlockSpec(memory_space=pltpu.SMEM), vmem, vmem),
        scratch_shapes=[
            pltpu.VMEM((CORES, own, half + LANES), BF16),
            pltpu.VMEM((n_q, own, half + LANES), BF16),
            pltpu.VMEM((n_p, own, half), BF16),
            pltpu.VMEM((n_q * own, half + LANES), F32),
            pltpu.VMEM((n_p * own, half), F32),
            pltpu.VMEM((n_p * own, n_q * own), F32),
            pltpu.VMEM((n_p * own, n_q * own), F32),
            pltpu.VMEM((PLANE, 8, n_q * own), F32),
            pltpu.VMEM((8, n_q * own), F32),
            pltpu.VMEM((n_q, own, half), BF16),
            pltpu.VMEM((PLANE, CORES, own, half), BF16),
            pltpu.VMEM((n_p, own, half), BF16),
            pltpu.VMEM((Z, CORES, own, half), BF16),
            pltpu.VMEM((Z, 8, n_q * own), F32),
            pltpu.VMEM((8, n_q * own), F32),
            pltpu.SemaphoreType.DMA((4,)),
            pltpu.SemaphoreType.DMA((7,)),
            pltpu.SemaphoreType.DMA((7,)),
        ],
        compiler_params=pltpu.CompilerParams(
            collective_id=0, has_side_effects=True, vmem_limit_bytes=32 * 1024 * 1024),
    )(queries, passages, positive)
    return loss[0, 0], gq, gp


def solution(mesh):
    placed = (P(("row", "col"), None), P(("row", "col"), None), P(("row", "col")))
    return jax.shard_map(
        per_device,
        mesh=mesh,
        in_specs=placed,
        out_specs=(P(), P(("row", "col"), None), P(("row", "col"), None)),
        check_vma=False,
    )
```

```python
import functools

import jax
import jax.numpy as jnp
from jax import lax
from jax.experimental import pallas as pl
from jax.experimental.pallas import tpu as pltpu
from jax.sharding import PartitionSpec as P

MESH = pl.DeviceIdType.MESH
X, Y, Z, CORES = 4, 4, 8, 2
PLANE = X * Y
LANES = 128
F32, BF16 = jnp.float32, jnp.bfloat16


def ring(step, n):
    return min(step, n - step)


PLANE_STEPS = sorted(
    ((dx, dy) for dx in range(X) for dy in range(Y) if dx or dy),
    key=lambda s: -(ring(s[0], X) + ring(s[1], Y)))
LINE_STEPS = sorted(range(1, Z), key=lambda s: -ring(s, Z))


def device_of(x, y, z, core):
    return (x * 2 + y % 2, z * 4 + (y // 2) * 2 + core)


def kernel(total, q_hbm, p_hbm, pos_hbm, loss_ref, g_ref,
           pos, stage, p_own, qbuf, pbuf, qwide, pwide, half_own, half_other, statbuf, stat_own,
           gq_send, gq_recv, gp_send, gp_recv, lossbuf, loss_own,
           local_sem, send_sem, recv_sem):
    row, col = lax.axis_index("row"), lax.axis_index("col")
    x, z, core = row // 2, col // 4, col % 2
    y = ((col // 2) % 2) * 2 + row % 2
    chip = x * Y + y
    own = q_hbm.shape[0]
    half = q_hbm.shape[1] // CORES
    p_count, q_count = Z * CORES, PLANE * CORES
    q_slot, p_slot = chip * CORES + core, z * CORES + core
    other = device_of(x, y, z, 1 - core)
    plane = [((x + dx) % X, (y + dy) % Y) for dx, dy in PLANE_STEPS]
    line = [(z + dz) % Z for dz in LINE_STEPS]

    barrier = pltpu.get_barrier_semaphore()

    def greet(device):
        pl.semaphore_signal(barrier, inc=1, device_id=device, device_id_type=MESH)

    for pz in line:
        for c in range(CORES):
            greet(device_of(x, y, pz, c))
    for px, py in plane:
        for c in range(CORES):
            greet(device_of(px, py, z, c))
    greet(other)

    loads = [pltpu.make_async_copy(pos_hbm, pos, local_sem.at[4])]
    for h in range(CORES):
        part = pl.ds(h * half, half)
        loads.append(pltpu.make_async_copy(p_hbm.at[:, part], p_own.at[h], local_sem.at[5 + h]))
        loads.append(pltpu.make_async_copy(q_hbm.at[:, part], stage.at[h, :, pl.ds(0, half)], local_sem.at[7 + h]))
    for load in loads:
        load.start()
    loads[0].wait()
    lane = lax.broadcasted_iota(jnp.int32, (1, LANES), 1)
    codes = []
    for k in range(own):
        index = pos[k]
        codes.append(((lane == index // 32) | (lane == 32 + index % 32)).astype(F32))
    code = jnp.concatenate(codes, axis=0).astype(BF16)
    for load in loads[1:]:
        load.wait()
    for h in range(CORES):
        stage[h, :, half:] = code

    pl.semaphore_wait(barrier, (PLANE + Z - 1) * CORES - 1)

    def send(src, dst, to, kind):
        return pltpu.make_async_remote_copy(
            src_ref=src, dst_ref=dst, send_sem=send_sem.at[kind], recv_sem=recv_sem.at[kind],
            device_id=to, device_id_type=MESH)

    def gather_plane(px, py):
        for c in range(CORES):
            send(stage.at[c], qbuf.at[q_slot], device_of(px, py, z, c), 0).start()

    def gather_line(pz):
        for c in range(CORES):
            send(p_own.at[c], pbuf.at[p_slot], device_of(x, y, pz, c), 1).start()

    for k in range(PLANE - 1):
        gather_plane(*plane[k])
        if k % 2 == 0 and k // 2 < Z - 1:
            gather_line(line[k // 2])
    send(stage.at[1 - core], qbuf.at[q_slot], other, 0).start()
    send(p_own.at[1 - core], pbuf.at[p_slot], other, 1).start()
    own_q = pltpu.make_async_copy(stage.at[core], qbuf.at[q_slot], local_sem.at[0])
    own_p = pltpu.make_async_copy(p_own.at[core], pbuf.at[p_slot], local_sem.at[1])
    own_q.start()
    own_p.start()

    def wait_recv(ref, kind):
        pltpu.make_async_copy(ref, ref, recv_sem.at[kind]).wait()

    def wait_send(ref, kind):
        pltpu.make_async_copy(ref, ref, send_sem.at[kind]).wait()

    n_p = p_count * own
    slot = lax.broadcasted_iota(jnp.int32, (n_p, LANES), 0)
    p_row, p_col = device_of(x, y, slot // (CORES * own), (slot // own) % CORES)
    p_id = (p_row * 32 + p_col) * own + slot % own
    p_lane = lax.broadcasted_iota(jnp.int32, (n_p, LANES), 1)
    p_code = ((p_lane == p_id // 32) | (p_lane == 32 + p_id % 32)).astype(F32).astype(BF16)

    own_p.wait()
    own_q.wait()
    wait_recv(pbuf.at[pl.ds(0, p_count - 1)], 1)
    for s in range(p_count):
        pwide[s * own:(s + 1) * own, :] = pbuf[s].astype(F32)
    passages = pwide[...].astype(BF16)
    wait_recv(qbuf.at[pl.ds(0, q_count - 1)], 0)
    for s in range(q_count):
        qwide[s * own:(s + 1) * own, :] = qbuf[s].astype(F32)
    queries = qwide[:, :half].astype(BF16)
    q_code = qwide[:, half:].astype(BF16)

    contract_last = (((1,), (1,)), ((), ()))
    half_own[...] = lax.dot_general(passages, queries, contract_last, preferred_element_type=F32)
    trade = send(half_own, half_other, other, 2)
    trade.start()
    matched = lax.dot_general(p_code, q_code, contract_last, preferred_element_type=F32) > 1.5
    trade.wait()
    scores = half_own[...] + half_other[...]

    n_q = q_count * own
    peak = jnp.max(scores, axis=0, keepdims=True)
    stat_own[:, :n_q] = peak
    stat_own[:, n_q:2 * n_q] = jnp.sum(jnp.exp(scores - peak), axis=0, keepdims=True)
    stat_own[:, 2 * n_q:] = jnp.sum(jnp.where(matched, scores, 0.0), axis=0, keepdims=True)
    statbuf[pl.ds(chip, 1)] = stat_own[...][None]
    for px, py in plane:
        send(stat_own, statbuf.at[chip], device_of(px, py, z, core), 3).start()
    wait_recv(statbuf.at[pl.ds(0, PLANE - 1)], 3)
    stats = statbuf[...]
    peaks, sums, picks = stats[:, :, :n_q], stats[:, :, n_q:2 * n_q], stats[:, :, 2 * n_q:]
    row_peak = jnp.max(peaks, axis=0)
    totals = jnp.sum(sums * jnp.exp(peaks - row_peak[None]), axis=0)
    positive_score = jnp.sum(picks, axis=0)
    weights = (jnp.exp(scores - row_peak) / totals - matched.astype(F32)).astype(BF16)

    loss_own[...] = row_peak + jnp.log(totals) - positive_score
    lossbuf[pl.ds(z, 1)] = loss_own[...][None]
    for pz in line:
        send(loss_own, lossbuf.at[z], device_of(x, y, pz, core), 6).start()

    for at in range(0, half, 256):
        part = lax.dot_general(weights, passages[:, at:at + 256], (((0,), (0,)), ((), ())),
                               preferred_element_type=F32).astype(BF16)
        for s in range(q_count):
            gq_send[s, :, at:at + 256] = part[s * own:(s + 1) * own]
    for px, py in plane:
        for c in range(CORES):
            send(gq_send.at[(px * Y + py) * CORES + c], gq_recv.at[chip, core], device_of(px, py, z, c), 4).start()
    send(gq_send.at[chip * CORES + 1 - core], gq_recv.at[chip, core], other, 4).start()
    own_gq = pltpu.make_async_copy(gq_send.at[q_slot], gq_recv.at[chip, core], local_sem.at[2])
    own_gq.start()
    for at in range(0, half, 256):
        part = jnp.dot(weights, queries[:, at:at + 256], preferred_element_type=F32).astype(BF16)
        for s in range(p_count):
            gp_send[s, :, at:at + 256] = part[s * own:(s + 1) * own]
    for pz in line:
        for c in range(CORES):
            send(gp_send.at[pz * CORES + c], gp_recv.at[z, core], device_of(x, y, pz, c), 5).start()
    send(gp_send.at[z * CORES + 1 - core], gp_recv.at[z, core], other, 5).start()
    own_gp = pltpu.make_async_copy(gp_send.at[p_slot], gp_recv.at[z, core], local_sem.at[3])
    own_gp.start()

    wait_recv(lossbuf.at[pl.ds(0, Z - 1)], 6)
    loss_ref[0, 0] = jnp.sum(jnp.sum(lossbuf[...], axis=0)) / total

    own_gq.wait()
    wait_recv(gq_send.at[pl.ds(0, q_count - 1)], 4)
    for h in range(CORES):
        acc = gq_recv[0, h].astype(F32)
        for k in range(1, PLANE):
            acc += gq_recv[k, h].astype(F32)
        g_ref[0, :, h * half:(h + 1) * half] = acc.astype(BF16)
    own_gp.wait()
    wait_recv(gp_send.at[pl.ds(0, p_count - 1)], 5)
    for h in range(CORES):
        acc = gp_recv[0, h].astype(F32)
        for k in range(1, Z):
            acc += gp_recv[k, h].astype(F32)
        g_ref[1, :, h * half:(h + 1) * half] = acc.astype(BF16)

    wait_send(qbuf.at[pl.ds(0, q_count - 1)], 0)
    wait_send(pbuf.at[pl.ds(0, p_count - 1)], 1)
    wait_send(statbuf.at[pl.ds(0, PLANE - 1)], 3)
    wait_send(gq_send.at[pl.ds(0, q_count - 1)], 4)
    wait_send(gp_send.at[pl.ds(0, p_count - 1)], 5)
    wait_send(lossbuf.at[pl.ds(0, Z - 1)], 6)


def per_device(queries, passages, positive):
    own, width = queries.shape
    half = width // CORES
    n_q, n_p = PLANE * CORES, Z * CORES
    vmem, hbm = pl.BlockSpec(memory_space=pltpu.VMEM), pl.BlockSpec(memory_space=pltpu.HBM)
    loss, grads = pl.pallas_call(
        functools.partial(kernel, n_q * own * Z),
        out_shape=(
            jax.ShapeDtypeStruct((1, 1), F32),
            jax.ShapeDtypeStruct((2, own, width), BF16),
        ),
        in_specs=[hbm, hbm, hbm],
        out_specs=(pl.BlockSpec(memory_space=pltpu.SMEM), vmem),
        scratch_shapes=[
            pltpu.SMEM((own,), jnp.int32),
            pltpu.VMEM((CORES, own, half + LANES), BF16),
            pltpu.VMEM((CORES, own, half), BF16),
            pltpu.VMEM((n_q, own, half + LANES), BF16),
            pltpu.VMEM((n_p, own, half), BF16),
            pltpu.VMEM((n_q * own, half + LANES), F32),
            pltpu.VMEM((n_p * own, half), F32),
            pltpu.VMEM((n_p * own, n_q * own), F32),
            pltpu.VMEM((n_p * own, n_q * own), F32),
            pltpu.VMEM((PLANE, 1, 3 * n_q * own), F32),
            pltpu.VMEM((1, 3 * n_q * own), F32),
            pltpu.VMEM((n_q, own, half), BF16),
            pltpu.VMEM((PLANE, CORES, own, half), BF16),
            pltpu.VMEM((n_p, own, half), BF16),
            pltpu.VMEM((Z, CORES, own, half), BF16),
            pltpu.VMEM((Z, 1, n_q * own), F32),
            pltpu.VMEM((1, n_q * own), F32),
            pltpu.SemaphoreType.DMA((9,)),
            pltpu.SemaphoreType.DMA((7,)),
            pltpu.SemaphoreType.DMA((7,)),
        ],
        compiler_params=pltpu.CompilerParams(
            collective_id=0, has_side_effects=True, vmem_limit_bytes=32 * 1024 * 1024),
    )(*(pltpu.with_memory_space_constraint(a, pltpu.HBM) for a in (queries, passages, positive)))
    return loss[0, 0], grads[0].astype(BF16), grads[1].astype(BF16)


def solution(mesh):
    placed = (P(("row", "col"), None), P(("row", "col"), None), P(("row", "col")))
    return jax.shard_map(
        per_device,
        mesh=mesh,
        in_specs=placed,
        out_specs=(P(), P(("row", "col"), None), P(("row", "col"), None)),
        check_vma=False,
    )
```

```python
import functools

import jax
import jax.numpy as jnp
from jax import lax
from jax.experimental import pallas as pl
from jax.experimental.pallas import tpu as pltpu
from jax.sharding import PartitionSpec as P

MESH = pl.DeviceIdType.MESH
X, Y, Z, CORES = 4, 4, 8, 2
PLANE = X * Y
LANES = 128
F32, BF16 = jnp.float32, jnp.bfloat16


def ring(step, n):
    return min(step, n - step)


PLANE_STEPS = sorted(
    ((dx, dy) for dx in range(X) for dy in range(Y) if dx or dy),
    key=lambda s: -(ring(s[0], X) + ring(s[1], Y)))
LINE_STEPS = sorted(range(1, Z), key=lambda s: -ring(s, Z))


def kernel(total, q_hbm, p_hbm, pos_hbm, g_ref,
           pos, stage, p_own, qbuf, pbuf, qwide, pwide, half_own, half_other, statbuf, stat_own,
           gq_send, gq_recv, gp_send, gp_recv, lossbuf, loss_own,
           local_sem, send_sem, recv_sem):
    row, col = lax.axis_index("row"), lax.axis_index("col")
    x, z, core = row >> 1, col >> 2, col & 1
    y = (col & 2) + (row & 1)
    chip = x * Y + y
    own = q_hbm.shape[0]
    half = q_hbm.shape[1] // CORES
    p_count, q_count = Z * CORES, PLANE * CORES
    q_slot, p_slot = chip * CORES + core, z * CORES + core
    other = (row, col ^ 1)
    xs, ys = [(x + d) & (X - 1) for d in range(X)], [(y + d) & (Y - 1) for d in range(Y)]
    x_row, y_row = [px * 2 for px in xs], [py & 1 for py in ys]
    y_col = [z * 4 + (py & 2) for py in ys]
    x_slot, y_slot = [px * (Y * CORES) for px in xs], [py * CORES for py in ys]
    zs = [(z + d) & (Z - 1) for d in range(Z)]
    z_col, z_slot = [pz * 4 + (col & 2) for pz in zs], [pz * CORES for pz in zs]

    def on_plane(step, c):
        dx, dy = step
        return (x_row[dx] + y_row[dy], y_col[dy] + c)

    def on_line(step, c):
        return (row, z_col[step] + c)

    loads = [pltpu.make_async_copy(pos_hbm, pos, local_sem.at[4])]
    for h in range(CORES):
        part = pl.ds(h * half, half)
        loads.append(pltpu.make_async_copy(p_hbm.at[:, part], p_own.at[h], local_sem.at[5 + h]))
        loads.append(pltpu.make_async_copy(q_hbm.at[:, part], stage.at[h, :, pl.ds(0, half)], local_sem.at[7 + h]))
    for load in loads:
        load.start()
    barrier = pltpu.get_barrier_semaphore()

    def greet(device):
        pl.semaphore_signal(barrier, inc=1, device_id=device, device_id_type=MESH)

    for far in range(X // 2 + Y // 2, 0, -1):
        for c in range(CORES):
            for step in LINE_STEPS:
                if ring(step, Z) == far:
                    greet(on_line(step, c))
            for step in PLANE_STEPS:
                if ring(step[0], X) + ring(step[1], Y) == far:
                    greet(on_plane(step, c))
    greet(other)

    loads[0].wait()
    lane = lax.broadcasted_iota(jnp.int32, (1, LANES), 1)
    codes = []
    for k in range(own):
        index = pos[k]
        codes.append(((lane == index // 32) | (lane == 32 + index % 32)).astype(F32))
    code = jnp.concatenate(codes, axis=0).astype(BF16)
    for load in loads[1:]:
        load.wait()
    for h in range(CORES):
        stage[h, :, half:] = code

    pl.semaphore_wait(barrier, (PLANE + Z - 1) * CORES - 1)

    def send(src, dst, to, kind):
        return pltpu.make_async_remote_copy(
            src_ref=src, dst_ref=dst, send_sem=send_sem.at[kind], recv_sem=recv_sem.at[kind],
            device_id=to, device_id_type=MESH)

    for k in range(PLANE - 1):
        for c in range(CORES):
            send(stage.at[c], qbuf.at[q_slot], on_plane(PLANE_STEPS[k], c), 0).start()
        if k % 2 == 0 and k // 2 < Z - 1:
            for c in range(CORES):
                send(p_own.at[c], pbuf.at[p_slot], on_line(LINE_STEPS[k // 2], c), 1).start()
    send(stage.at[1 - core], qbuf.at[q_slot], other, 0).start()
    send(p_own.at[1 - core], pbuf.at[p_slot], other, 1).start()
    own_q = pltpu.make_async_copy(stage.at[core], qbuf.at[q_slot], local_sem.at[0])
    own_p = pltpu.make_async_copy(p_own.at[core], pbuf.at[p_slot], local_sem.at[1])
    own_q.start()
    own_p.start()

    def wait_recv(ref, kind):
        pltpu.make_async_copy(ref, ref, recv_sem.at[kind]).wait()

    def wait_send(ref, kind):
        pltpu.make_async_copy(ref, ref, send_sem.at[kind]).wait()

    n_p = p_count * own
    slot = lax.broadcasted_iota(jnp.int32, (n_p, LANES), 0)
    p_col = slot // (CORES * own) * 4 + (col & 2) + (slot // own) % CORES
    p_id = (row * 32 + p_col) * own + slot % own
    p_lane = lax.broadcasted_iota(jnp.int32, (n_p, LANES), 1)
    p_code = ((p_lane == p_id // 32) | (p_lane == 32 + p_id % 32)).astype(F32).astype(BF16)

    own_p.wait()
    own_q.wait()
    wait_recv(pbuf.at[pl.ds(0, p_count - 1)], 1)
    for s in range(p_count):
        pwide[s * own:(s + 1) * own, :] = pbuf[s].astype(F32)
    passages = pwide[...].astype(BF16)
    wait_recv(qbuf.at[pl.ds(0, q_count - 1)], 0)
    for s in range(q_count):
        qwide[s * own:(s + 1) * own, :] = qbuf[s].astype(F32)
    queries = qwide[:, :half].astype(BF16)
    q_code = qwide[:, half:].astype(BF16)

    contract_last = (((1,), (1,)), ((), ()))
    half_own[...] = lax.dot_general(passages, queries, contract_last, preferred_element_type=F32)
    trade = send(half_own, half_other, other, 2)
    trade.start()
    matched = lax.dot_general(p_code, q_code, contract_last, preferred_element_type=F32) > 1.5
    trade.wait()
    scores = half_own[...] + half_other[...]

    n_q = q_count * own
    peak = jnp.max(scores, axis=0, keepdims=True)
    stat_own[:, :n_q] = peak
    stat_own[:, n_q:2 * n_q] = jnp.sum(jnp.exp(scores - peak), axis=0, keepdims=True)
    stat_own[:, 2 * n_q:] = jnp.sum(jnp.where(matched, scores, 0.0), axis=0, keepdims=True)
    statbuf[pl.ds(chip, 1)] = stat_own[...][None]
    for step in PLANE_STEPS:
        send(stat_own, statbuf.at[chip], on_plane(step, core), 3).start()
    wait_recv(statbuf.at[pl.ds(0, PLANE - 1)], 3)
    stats = statbuf[...]
    peaks, sums, picks = stats[:, :, :n_q], stats[:, :, n_q:2 * n_q], stats[:, :, 2 * n_q:]
    row_peak = jnp.max(peaks, axis=0)
    totals = jnp.sum(sums * jnp.exp(peaks - row_peak[None]), axis=0)
    positive_score = jnp.sum(picks, axis=0)
    weights = (jnp.exp(scores - row_peak) / totals - matched.astype(F32)).astype(BF16)

    loss_own[...] = row_peak + jnp.log(totals) - positive_score
    lossbuf[pl.ds(z, 1)] = loss_own[...][None]
    for step in LINE_STEPS:
        send(loss_own, lossbuf.at[z], on_line(step, core), 6).start()

    for at in range(0, half, 256):
        part = jnp.dot(weights, queries[:, at:at + 256], preferred_element_type=F32).astype(BF16)
        for s in range(p_count):
            gp_send[s, :, at:at + 256] = part[s * own:(s + 1) * own]
    for step in LINE_STEPS:
        for c in range(CORES):
            send(gp_send.at[z_slot[step] + c], gp_recv.at[z, core], on_line(step, c), 5).start()
    send(gp_send.at[z * CORES + 1 - core], gp_recv.at[z, core], other, 5).start()
    own_gp = pltpu.make_async_copy(gp_send.at[p_slot], gp_recv.at[z, core], local_sem.at[3])
    own_gp.start()

    for at in range(0, half, 256):
        part = lax.dot_general(weights, passages[:, at:at + 256], (((0,), (0,)), ((), ())),
                               preferred_element_type=F32).astype(BF16)
        for s in range(q_count):
            gq_send[s, :, at:at + 256] = part[s * own:(s + 1) * own]
    for step in PLANE_STEPS:
        for c in range(CORES):
            send(gq_send.at[x_slot[step[0]] + y_slot[step[1]] + c], gq_recv.at[chip, core], on_plane(step, c), 4).start()
    send(gq_send.at[chip * CORES + 1 - core], gq_recv.at[chip, core], other, 4).start()
    own_gq = pltpu.make_async_copy(gq_send.at[q_slot], gq_recv.at[chip, core], local_sem.at[2])
    own_gq.start()
    wait_recv(lossbuf.at[pl.ds(0, Z - 1)], 6)
    loss = jnp.sum(jnp.sum(lossbuf[...], axis=0)) / total
    at_first = (lax.broadcasted_iota(jnp.int32, (own, LANES), 0) == 0) & (lax.broadcasted_iota(jnp.int32, (own, LANES), 1) == 0)
    g_ref[2] = jnp.zeros(g_ref.shape[1:], F32)
    g_ref[2, :, :LANES] = jnp.where(at_first, loss, 0.0)

    own_gq.wait()
    wait_recv(gq_send.at[pl.ds(0, q_count - 1)], 4)
    for h in range(CORES):
        acc = gq_recv[0, h].astype(F32)
        for k in range(1, PLANE):
            acc += gq_recv[k, h].astype(F32)
        g_ref[0, :, h * half:(h + 1) * half] = acc
    own_gp.wait()
    wait_recv(gp_send.at[pl.ds(0, p_count - 1)], 5)
    for h in range(CORES):
        acc = gp_recv[0, h].astype(F32)
        for k in range(1, Z):
            acc += gp_recv[k, h].astype(F32)
        g_ref[1, :, h * half:(h + 1) * half] = acc

    wait_send(qbuf.at[pl.ds(0, q_count - 1)], 0)
    wait_send(pbuf.at[pl.ds(0, p_count - 1)], 1)
    wait_send(statbuf.at[pl.ds(0, PLANE - 1)], 3)
    wait_send(gq_send.at[pl.ds(0, q_count - 1)], 4)
    wait_send(gp_send.at[pl.ds(0, p_count - 1)], 5)
    wait_send(lossbuf.at[pl.ds(0, Z - 1)], 6)


def hand_out(all_ref, loss_out, gq_out, gp_out, narrow, sem):
    narrow[...] = all_ref[:2].astype(BF16)
    copies = (pltpu.make_async_copy(all_ref.at[2, pl.ds(0, 1), pl.ds(0, LANES)], loss_out, sem.at[2]),
              pltpu.make_async_copy(narrow.at[0], gq_out, sem.at[0]), pltpu.make_async_copy(narrow.at[1], gp_out, sem.at[1]))
    for copy in copies:
        copy.start()
    for copy in copies:
        copy.wait()


def per_device(queries, passages, positive):
    own, width = queries.shape
    half = width // CORES
    n_q, n_p = PLANE * CORES, Z * CORES
    vmem, hbm = pl.BlockSpec(memory_space=pltpu.VMEM), pl.BlockSpec(memory_space=pltpu.HBM)
    out = pl.pallas_call(
        functools.partial(kernel, n_q * own * Z),
        out_shape=jax.ShapeDtypeStruct((3, own, width), F32),
        in_specs=[hbm, hbm, hbm],
        out_specs=vmem,
        scratch_shapes=[
            pltpu.SMEM((own,), jnp.int32),
            pltpu.VMEM((CORES, own, half + LANES), BF16),
            pltpu.VMEM((CORES, own, half), BF16),
            pltpu.VMEM((n_q, own, half + LANES), BF16),
            pltpu.VMEM((n_p, own, half), BF16),
            pltpu.VMEM((n_q * own, half + LANES), F32),
            pltpu.VMEM((n_p * own, half), F32),
            pltpu.VMEM((n_p * own, n_q * own), F32),
            pltpu.VMEM((n_p * own, n_q * own), F32),
            pltpu.VMEM((PLANE, 1, 3 * n_q * own), F32),
            pltpu.VMEM((1, 3 * n_q * own), F32),
            pltpu.VMEM((n_q, own, half), BF16),
            pltpu.VMEM((PLANE, CORES, own, half), BF16),
            pltpu.VMEM((n_p, own, half), BF16),
            pltpu.VMEM((Z, CORES, own, half), BF16),
            pltpu.VMEM((Z, 1, n_q * own), F32),
            pltpu.VMEM((1, n_q * own), F32),
            pltpu.SemaphoreType.DMA((9,)),
            pltpu.SemaphoreType.DMA((7,)),
            pltpu.SemaphoreType.DMA((7,)),
        ],
        compiler_params=pltpu.CompilerParams(
            collective_id=0, has_side_effects=True, vmem_limit_bytes=32 * 1024 * 1024),
    )(*(pltpu.with_memory_space_constraint(a, pltpu.HBM) for a in (queries, passages, positive)))
    loss, gq, gp = pl.pallas_call(
        hand_out,
        out_shape=(
            jax.ShapeDtypeStruct((1, LANES), F32),
            jax.ShapeDtypeStruct((own, width), BF16),
            jax.ShapeDtypeStruct((own, width), BF16),
        ),
        in_specs=[vmem],
        out_specs=(hbm, hbm, hbm),
        scratch_shapes=[pltpu.VMEM((2, own, width), BF16), pltpu.SemaphoreType.DMA((3,))],
    )(pltpu.with_memory_space_constraint(out, pltpu.VMEM))
    return loss[0, 0], gq, gp


def solution(mesh):
    placed = (P(("row", "col"), None), P(("row", "col"), None), P(("row", "col")))
    return jax.shard_map(
        per_device,
        mesh=mesh,
        in_specs=placed,
        out_specs=(P(), P(("row", "col"), None), P(("row", "col"), None)),
        check_vma=False,
    )
```

```python
import functools

import jax
import jax.numpy as jnp
from jax import lax
from jax.experimental import pallas as pl
from jax.experimental.pallas import tpu as pltpu
from jax.sharding import PartitionSpec as P

MESH = pl.DeviceIdType.MESH
X, Y, Z, CORES = 4, 4, 8, 2
PLANE = X * Y
LANES = 128
F32, BF16 = jnp.float32, jnp.bfloat16


def ring(step, n):
    return min(step, n - step)


PLANE_STEPS = sorted(
    ((dx, dy) for dx in range(X) for dy in range(Y) if dx or dy),
    key=lambda s: -(ring(s[0], X) + ring(s[1], Y)))
LINE_STEPS = sorted(range(1, Z), key=lambda s: -ring(s, Z))


def kernel(total, q_hbm, p_hbm, pos_hbm, g_ref,
           pos, stage, p_own, qbuf, pbuf, qwide, pwide, half_own, half_other, statbuf, stat_own,
           gq_send, gq_recv, gp_send, gp_recv, lossbuf, loss_own,
           local_sem, send_sem, recv_sem):
    row, col = lax.axis_index("row"), lax.axis_index("col")
    x, z, core = row >> 1, col >> 2, col & 1
    y = (col & 2) + (row & 1)
    chip = x * Y + y
    own = q_hbm.shape[0]
    half = q_hbm.shape[1] // CORES
    q_count, p_count = Z * CORES, PLANE * CORES
    p_slot, q_slot = chip * CORES + core, z * CORES + core
    other = (row, col ^ 1)
    xs, ys = [(x + d) & (X - 1) for d in range(X)], [(y + d) & (Y - 1) for d in range(Y)]
    x_row, y_row = [px * 2 for px in xs], [py & 1 for py in ys]
    y_col = [z * 4 + (py & 2) for py in ys]
    x_slot, y_slot = [px * (Y * CORES) for px in xs], [py * CORES for py in ys]
    zs = [(z + d) & (Z - 1) for d in range(Z)]
    z_col, z_slot = [pz * 4 + (col & 2) for pz in zs], [pz * CORES for pz in zs]

    def on_plane(step, c):
        dx, dy = step
        return (x_row[dx] + y_row[dy], y_col[dy] + c)

    def on_line(step, c):
        return (row, z_col[step] + c)

    loads = [pltpu.make_async_copy(pos_hbm, pos, local_sem.at[4])]
    for h in range(CORES):
        part = pl.ds(h * half, half)
        loads.append(pltpu.make_async_copy(p_hbm.at[:, part], p_own.at[h], local_sem.at[5 + h]))
        loads.append(pltpu.make_async_copy(q_hbm.at[:, part], stage.at[h, :, pl.ds(0, half)], local_sem.at[7 + h]))
    for load in loads:
        load.start()
    barrier = pltpu.get_barrier_semaphore()

    def greet(device):
        pl.semaphore_signal(barrier, inc=1, device_id=device, device_id_type=MESH)

    for far in range(X // 2 + Y // 2, 0, -1):
        for c in range(CORES):
            for step in LINE_STEPS:
                if ring(step, Z) == far:
                    greet(on_line(step, c))
            for step in PLANE_STEPS:
                if ring(step[0], X) + ring(step[1], Y) == far:
                    greet(on_plane(step, c))
    greet(other)

    loads[0].wait()
    lane = lax.broadcasted_iota(jnp.int32, (1, LANES), 1)
    codes = []
    for k in range(own):
        index = pos[k]
        codes.append(((lane == index // 32) | (lane == 32 + index % 32)).astype(F32))
    code = jnp.concatenate(codes, axis=0).astype(BF16)
    for load in loads[1:]:
        load.wait()
    for h in range(CORES):
        stage[h, :, half:] = code

    pl.semaphore_wait(barrier, (PLANE + Z - 1) * CORES - 1)

    def send(src, dst, to, kind):
        return pltpu.make_async_remote_copy(
            src_ref=src, dst_ref=dst, send_sem=send_sem.at[kind], recv_sem=recv_sem.at[kind],
            device_id=to, device_id_type=MESH)

    for k in range(PLANE - 1):
        for c in range(CORES):
            send(p_own.at[c], pbuf.at[p_slot], on_plane(PLANE_STEPS[k], c), 1).start()
        if k % 2 == 0 and k // 2 < Z - 1:
            for c in range(CORES):
                send(stage.at[c], qbuf.at[q_slot], on_line(LINE_STEPS[k // 2], c), 0).start()
    send(stage.at[1 - core], qbuf.at[q_slot], other, 0).start()
    send(p_own.at[1 - core], pbuf.at[p_slot], other, 1).start()
    own_q = pltpu.make_async_copy(stage.at[core], qbuf.at[q_slot], local_sem.at[0])
    own_p = pltpu.make_async_copy(p_own.at[core], pbuf.at[p_slot], local_sem.at[1])
    own_q.start()
    own_p.start()

    def wait_recv(ref, kind):
        pltpu.make_async_copy(ref, ref, recv_sem.at[kind]).wait()

    def wait_send(ref, kind):
        pltpu.make_async_copy(ref, ref, send_sem.at[kind]).wait()

    n_p = p_count * own
    slot = lax.broadcasted_iota(jnp.int32, (n_p, LANES), 0)
    p_chip = slot // (CORES * own)
    p_row = p_chip // Y * 2 + p_chip % 2
    p_col = z * 4 + p_chip % Y // 2 * 2 + slot // own % CORES
    p_id = (p_row * 32 + p_col) * own + slot % own
    p_lane = lax.broadcasted_iota(jnp.int32, (n_p, LANES), 1)
    p_code = ((p_lane == p_id // 32) | (p_lane == 32 + p_id % 32)).astype(F32).astype(BF16)

    own_p.wait()
    own_q.wait()
    wait_recv(pbuf.at[pl.ds(0, p_count - 1)], 1)
    for s in range(p_count):
        pwide[s * own:(s + 1) * own, :] = pbuf[s].astype(F32)
    passages = pwide[...].astype(BF16)
    wait_recv(qbuf.at[pl.ds(0, q_count - 1)], 0)
    for s in range(q_count):
        qwide[s * own:(s + 1) * own, :] = qbuf[s].astype(F32)
    queries = qwide[:, :half].astype(BF16)
    q_code = qwide[:, half:].astype(BF16)

    contract_last = (((1,), (1,)), ((), ()))
    half_own[...] = lax.dot_general(passages, queries, contract_last, preferred_element_type=F32)
    trade = send(half_own, half_other, other, 2)
    trade.start()
    matched = lax.dot_general(p_code, q_code, contract_last, preferred_element_type=F32) > 1.5
    trade.wait()
    scores = half_own[...] + half_other[...]

    n_q = q_count * own
    peak = jnp.max(scores, axis=0, keepdims=True)
    stat_own[:, :n_q] = peak
    stat_own[:, LANES:LANES + n_q] = jnp.sum(jnp.exp(scores - peak), axis=0, keepdims=True)
    stat_own[:, 2 * LANES:2 * LANES + n_q] = jnp.sum(jnp.where(matched, scores, 0.0), axis=0, keepdims=True)
    statbuf[pl.ds(z, 1)] = stat_own[...][None]
    for step in LINE_STEPS:
        send(stat_own, statbuf.at[z], on_line(step, core), 3).start()
    wait_recv(statbuf.at[pl.ds(0, Z - 1)], 3)
    stats = statbuf[...]
    peaks, sums, picks = stats[:, :, :n_q], stats[:, :, LANES:LANES + n_q], stats[:, :, 2 * LANES:2 * LANES + n_q]
    row_peak = jnp.max(peaks, axis=0)
    totals = jnp.sum(sums * jnp.exp(peaks - row_peak[None]), axis=0)
    positive_score = jnp.sum(picks, axis=0)
    weights = (jnp.exp(scores - row_peak) / totals - matched.astype(F32)).astype(BF16)

    loss_own[...] = jnp.zeros_like(loss_own)
    loss_own[:, :n_q] = row_peak + jnp.log(totals) - positive_score
    lossbuf[pl.ds(chip, 1)] = loss_own[...][None]
    for step in PLANE_STEPS:
        send(loss_own, lossbuf.at[chip], on_plane(step, core), 6).start()

    for at in range(0, half, 256):
        part = jnp.dot(weights, queries[:, at:at + 256], preferred_element_type=F32).astype(BF16)
        for s in range(p_count):
            gp_send[s, :, at:at + 256] = part[s * own:(s + 1) * own]
    for step in PLANE_STEPS:
        for c in range(CORES):
            send(gp_send.at[x_slot[step[0]] + y_slot[step[1]] + c], gp_recv.at[chip, core], on_plane(step, c), 5).start()
    send(gp_send.at[chip * CORES + 1 - core], gp_recv.at[chip, core], other, 5).start()
    own_gp = pltpu.make_async_copy(gp_send.at[p_slot], gp_recv.at[chip, core], local_sem.at[3])
    own_gp.start()
    for at in range(0, half, 256):
        part = lax.dot_general(weights, passages[:, at:at + 256], (((0,), (0,)), ((), ())),
                               preferred_element_type=F32).astype(BF16)
        for s in range(q_count):
            gq_send[s, :, at:at + 256] = part[s * own:(s + 1) * own]
    for step in LINE_STEPS:
        for c in range(CORES):
            send(gq_send.at[z_slot[step] + c], gq_recv.at[z, core], on_line(step, c), 4).start()
    send(gq_send.at[z * CORES + 1 - core], gq_recv.at[z, core], other, 4).start()
    own_gq = pltpu.make_async_copy(gq_send.at[q_slot], gq_recv.at[z, core], local_sem.at[2])
    own_gq.start()

    wait_recv(lossbuf.at[pl.ds(0, PLANE - 1)], 6)
    loss = jnp.sum(jnp.sum(lossbuf[...], axis=0)) / total
    at_first = (lax.broadcasted_iota(jnp.int32, (own, LANES), 0) == 0) & (lax.broadcasted_iota(jnp.int32, (own, LANES), 1) == 0)
    g_ref[2] = jnp.zeros(g_ref.shape[1:], F32)
    g_ref[2, :, :LANES] = jnp.where(at_first, loss, 0.0)

    own_gq.wait()
    wait_recv(gq_send.at[pl.ds(0, q_count - 1)], 4)
    for h in range(CORES):
        acc = gq_recv[0, h].astype(F32)
        for k in range(1, Z):
            acc += gq_recv[k, h].astype(F32)
        g_ref[0, :, h * half:(h + 1) * half] = acc
    own_gp.wait()
    wait_recv(gp_send.at[pl.ds(0, p_count - 1)], 5)
    for h in range(CORES):
        acc = gp_recv[0, h].astype(F32)
        for k in range(1, PLANE):
            acc += gp_recv[k, h].astype(F32)
        g_ref[1, :, h * half:(h + 1) * half] = acc

    wait_send(qbuf.at[pl.ds(0, q_count - 1)], 0)
    wait_send(pbuf.at[pl.ds(0, p_count - 1)], 1)
    wait_send(statbuf.at[pl.ds(0, Z - 1)], 3)
    wait_send(gq_send.at[pl.ds(0, q_count - 1)], 4)
    wait_send(gp_send.at[pl.ds(0, p_count - 1)], 5)
    wait_send(lossbuf.at[pl.ds(0, PLANE - 1)], 6)


def hand_out(all_ref, loss_out, gq_out, gp_out, narrow, sem):
    narrow[...] = all_ref[:2].astype(BF16)
    copies = (pltpu.make_async_copy(all_ref.at[2, pl.ds(0, 1), pl.ds(0, LANES)], loss_out, sem.at[2]),
              pltpu.make_async_copy(narrow.at[0], gq_out, sem.at[0]), pltpu.make_async_copy(narrow.at[1], gp_out, sem.at[1]))
    for copy in copies:
        copy.start()
    for copy in copies:
        copy.wait()


def per_device(queries, passages, positive):
    own, width = queries.shape
    half = width // CORES
    n_q, n_p = Z * CORES, PLANE * CORES
    vmem, hbm = pl.BlockSpec(memory_space=pltpu.VMEM), pl.BlockSpec(memory_space=pltpu.HBM)
    out = pl.pallas_call(
        functools.partial(kernel, n_q * own * PLANE),
        out_shape=jax.ShapeDtypeStruct((3, own, width), F32),
        in_specs=[hbm, hbm, hbm],
        out_specs=vmem,
        scratch_shapes=[
            pltpu.SMEM((own,), jnp.int32),
            pltpu.VMEM((CORES, own, half + LANES), BF16),
            pltpu.VMEM((CORES, own, half), BF16),
            pltpu.VMEM((n_q, own, half + LANES), BF16),
            pltpu.VMEM((n_p, own, half), BF16),
            pltpu.VMEM((n_q * own, half + LANES), F32),
            pltpu.VMEM((n_p * own, half), F32),
            pltpu.VMEM((n_p * own, n_q * own), F32),
            pltpu.VMEM((n_p * own, n_q * own), F32),
            pltpu.VMEM((Z, 1, 3 * LANES), F32),
            pltpu.VMEM((1, 3 * LANES), F32),
            pltpu.VMEM((n_q, own, half), BF16),
            pltpu.VMEM((Z, CORES, own, half), BF16),
            pltpu.VMEM((n_p, own, half), BF16),
            pltpu.VMEM((PLANE, CORES, own, half), BF16),
            pltpu.VMEM((PLANE, 1, LANES), F32),
            pltpu.VMEM((1, LANES), F32),
            pltpu.SemaphoreType.DMA((9,)),
            pltpu.SemaphoreType.DMA((7,)),
            pltpu.SemaphoreType.DMA((7,)),
        ],
        compiler_params=pltpu.CompilerParams(
            collective_id=0, has_side_effects=True, vmem_limit_bytes=32 * 1024 * 1024),
    )(*(pltpu.with_memory_space_constraint(a, pltpu.HBM) for a in (queries, passages, positive)))
    loss, gq, gp = pl.pallas_call(
        hand_out,
        out_shape=(
            jax.ShapeDtypeStruct((1, LANES), F32),
            jax.ShapeDtypeStruct((own, width), BF16),
            jax.ShapeDtypeStruct((own, width), BF16),
        ),
        in_specs=[vmem],
        out_specs=(hbm, hbm, hbm),
        scratch_shapes=[pltpu.VMEM((2, own, width), BF16), pltpu.SemaphoreType.DMA((3,))],
    )(pltpu.with_memory_space_constraint(out, pltpu.VMEM))
    return loss[0, 0], gq, gp


def solution(mesh):
    placed = (P(("row", "col"), None), P(("row", "col"), None), P(("row", "col")))
    return jax.shard_map(
        per_device,
        mesh=mesh,
        in_specs=placed,
        out_specs=(P(), P(("row", "col"), None), P(("row", "col"), None)),
        check_vma=False,
    )
```

```python
import functools

import jax
import jax.numpy as jnp
from jax import lax
from jax.experimental import pallas as pl
from jax.experimental.pallas import tpu as pltpu
from jax.sharding import PartitionSpec as P

MESH = pl.DeviceIdType.MESH
X, Y, Z, CORES = 4, 4, 8, 2
PLANE = X * Y
LANES = 128
F32, BF16 = jnp.float32, jnp.bfloat16


def ring(step, n):
    return min(step, n - step)


PLANE_STEPS = sorted(
    ((dx, dy) for dx in range(X) for dy in range(Y) if dx or dy),
    key=lambda s: -(ring(s[0], X) + ring(s[1], Y)))
LINE_STEPS = sorted(range(1, Z), key=lambda s: -ring(s, Z))


def kernel(total, q_hbm, p_hbm, pos_hbm, g_ref,
           pos, stage, p_own, qbuf, pbuf, qwide, pwide, statbuf, stat_own,
           gp_send, gp_recv, p_other, score_own, score_other, gq_send, gq_recv, lossbuf, loss_own,
           local_sem, send_sem, recv_sem, land_sem):
    row, col = lax.axis_index("row"), lax.axis_index("col")
    x, z, core = row >> 1, col >> 2, col & 1
    y = (col & 2) + (row & 1)
    chip = x * Y + y
    own, width = q_hbm.shape
    half = width // 2
    q_slot = core * Z + z
    other = (row, col ^ 1)
    xs, ys = [(x + d) & (X - 1) for d in range(X)], [(y + d) & (Y - 1) for d in range(Y)]
    x_row, y_row = [px * 2 for px in xs], [py & 1 for py in ys]
    y_col = [z * 4 + (py & 2) for py in ys]
    x_slot = [px * Y for px in xs]
    zs = [(z + d) & (Z - 1) for d in range(Z)]
    z_col = [pz * 4 + (col & 2) for pz in zs]

    def on_plane(step):
        dx, dy = step
        return (x_row[dx] + y_row[dy], y_col[dy] + core)

    def on_line(step, c):
        return (row, z_col[step] + c)

    loads = [
        pltpu.make_async_copy(pos_hbm, pos, local_sem.at[0]),
        pltpu.make_async_copy(p_hbm, p_own, local_sem.at[1]),
        pltpu.make_async_copy(q_hbm, stage.at[:, pl.ds(0, width)], local_sem.at[2]),
    ]
    for load in loads:
        load.start()
    barrier = pltpu.get_barrier_semaphore()

    def greet(device):
        pl.semaphore_signal(barrier, inc=1, device_id=device, device_id_type=MESH)

    for far in range(X // 2 + Y // 2, 0, -1):
        for step in PLANE_STEPS:
            if ring(step[0], X) + ring(step[1], Y) == far:
                greet(on_plane(step))
        for step in LINE_STEPS:
            if ring(step, Z) == far:
                for c in range(CORES):
                    greet(on_line(step, c))
    greet(other)

    loads[0].wait()
    lane = lax.broadcasted_iota(jnp.int32, (1, LANES), 1)
    codes = []
    for k in range(own):
        index = pos[k]
        codes.append(((lane == index // 32) | (lane == 32 + index % 32)).astype(F32))
    code = jnp.concatenate(codes, axis=0).astype(BF16)
    for load in loads[1:]:
        load.wait()
    stage[:, width:] = code

    pl.semaphore_wait(barrier, PLANE - 1 + (Z - 1) * CORES + 1)

    def send(src, dst, to, kind, landed=None):
        return pltpu.make_async_remote_copy(
            src_ref=src, dst_ref=dst, send_sem=send_sem.at[kind],
            recv_sem=recv_sem.at[kind] if landed is None else landed,
            device_id=to, device_id_type=MESH)

    for step in LINE_STEPS:
        send(stage, qbuf.at[q_slot], on_line(step, core), 0, land_sem.at[step]).start()
    for step in PLANE_STEPS:
        send(p_own, pbuf.at[chip], on_plane(step), 1).start()
    send(stage, qbuf.at[q_slot], other, 2).start()
    own_q = pltpu.make_async_copy(stage, qbuf.at[q_slot], local_sem.at[3])
    own_p = pltpu.make_async_copy(p_own, pbuf.at[chip], local_sem.at[4])
    own_q.start()
    own_p.start()

    def wait_recv(ref, kind):
        pltpu.make_async_copy(ref, ref, recv_sem.at[kind]).wait()

    def wait_send(ref, kind):
        pltpu.make_async_copy(ref, ref, send_sem.at[kind]).wait()

    p_count, q_count = PLANE, Z * CORES
    n_p, n_q = p_count * own, q_count * own
    slot = lax.broadcasted_iota(jnp.int32, (n_p, LANES), 0)
    p_chip = slot // own
    p_row = p_chip // Y * 2 + p_chip % 2
    p_lane = lax.broadcasted_iota(jnp.int32, (n_p, LANES), 1)

    def passage_code(c):
        p_id = (p_row * 32 + z * 4 + p_chip % Y // 2 * 2 + c) * own + slot % own
        return ((p_lane == p_id // 32) | (p_lane == 32 + p_id % 32)).astype(F32).astype(BF16)

    for step in LINE_STEPS[::-1]:
        landed = qbuf.at[core * Z + zs[Z - step]]
        pltpu.make_async_copy(landed, landed, land_sem.at[step]).wait()
        send(landed, landed, other, 2).start()
    own_p.wait()
    own_q.wait()
    wait_recv(pbuf.at[pl.ds(0, p_count - 1)], 1)
    give_passages = send(pbuf, p_other, other, 7)
    give_passages.start()
    for s in range(p_count):
        pwide[s * own:(s + 1) * own, :] = pbuf[s].astype(F32)
    passages = pwide[...].astype(BF16)
    wait_recv(qbuf.at[pl.ds(0, Z)], 2)
    for s in range(q_count):
        qwide[s * own:(s + 1) * own, :] = qbuf[s].astype(F32)
    queries = qwide[:, :width].astype(BF16)
    q_code = qwide[:, width:].astype(BF16)

    contract_last = (((1,), (1,)), ((), ()))
    scores = lax.dot_general(passages, queries, contract_last, preferred_element_type=F32)

    def match(c):
        return lax.dot_general(passage_code(c), q_code, contract_last, preferred_element_type=F32) > 1.5

    matched = match(core)

    peak = jnp.max(scores, axis=0, keepdims=True)
    stat_own[:, :n_q] = peak
    stat_own[:, LANES:LANES + n_q] = jnp.sum(jnp.exp(scores - peak), axis=0, keepdims=True)
    stat_own[:, 2 * LANES:2 * LANES + n_q] = jnp.sum(jnp.where(matched, scores, 0.0), axis=0, keepdims=True)
    statbuf[pl.ds(q_slot, 1)] = stat_own[...][None]
    for step in LINE_STEPS:
        for c in range(CORES):
            send(stat_own, statbuf.at[q_slot], on_line(step, c), 3).start()
    send(stat_own, statbuf.at[q_slot], other, 3).start()
    score_own[...] = scores
    give_scores = send(score_own, score_other, other, 8)
    give_scores.start()
    matched_other = match(1 - core)
    give_passages.wait()
    for s in range(p_count):
        pwide[s * own:(s + 1) * own, :] = p_other[s].astype(F32)
    passages_other = pwide[...].astype(BF16)
    give_scores.wait()
    wait_recv(statbuf.at[pl.ds(0, q_count - 1)], 3)
    stats = statbuf[...]
    peaks, sums, picks = stats[:, :, :n_q], stats[:, :, LANES:LANES + n_q], stats[:, :, 2 * LANES:2 * LANES + n_q]
    row_peak = jnp.max(peaks, axis=0)
    totals = jnp.sum(sums * jnp.exp(peaks - row_peak[None]), axis=0)
    positive_score = jnp.sum(picks, axis=0)

    def weigh(block, match):
        return jnp.exp(block - row_peak) / totals - match.astype(F32)

    wide = weigh(scores, matched)
    weights = wide.astype(BF16)

    loss_own[...] = jnp.zeros_like(loss_own)
    loss_own[:, :n_q] = row_peak + jnp.log(totals) - positive_score
    lossbuf[pl.ds(chip, 1)] = loss_own[...][None]
    for step in PLANE_STEPS:
        send(loss_own, lossbuf.at[chip], on_plane(step), 6).start()
    for at in range(0, width, 256):
        part = jnp.dot(weights, queries[:, at:at + 256], preferred_element_type=F32).astype(BF16)
        for s in range(p_count):
            gp_send[s, :, at:at + 256] = part[s * own:(s + 1) * own]
    for step in PLANE_STEPS:
        send(gp_send.at[x_slot[step[0]] + ys[step[1]]], gp_recv.at[chip], on_plane(step), 4).start()
    own_gp = pltpu.make_async_copy(gp_send.at[chip], gp_recv.at[chip], local_sem.at[5])
    own_gp.start()

    def of_mine(w):
        return jnp.where(core == 0, w[:, :n_q // 2], w[:, n_q // 2:]).astype(BF16)

    w_own, w_other = of_mine(wide), of_mine(weigh(score_other[...], matched_other))

    def share(w, block):
        return lax.dot_general(w, block, (((0,), (0,)), ((), ())), preferred_element_type=F32)

    for at in range(0, width, 256):
        part = (share(w_own, passages[:, at:at + 256]) + share(w_other, passages_other[:, at:at + 256])).astype(BF16)
        for s in range(Z):
            gq_send[s, :, at:at + 256] = part[s * own:(s + 1) * own]
    for step in LINE_STEPS:
        send(gq_send.at[zs[step]], gq_recv.at[z], on_line(step, core), 5).start()
    own_gq = pltpu.make_async_copy(gq_send.at[z], gq_recv.at[z], local_sem.at[6])
    own_gq.start()

    wait_recv(lossbuf.at[pl.ds(0, PLANE - 1)], 6)
    loss = jnp.sum(jnp.sum(lossbuf[...], axis=0)) / total
    at_first = (lax.broadcasted_iota(jnp.int32, (own, LANES), 0) == 0) & (lax.broadcasted_iota(jnp.int32, (own, LANES), 1) == 0)
    g_ref[2] = jnp.zeros(g_ref.shape[1:], F32)
    g_ref[2, :, :LANES] = jnp.where(at_first, loss, 0.0)

    own_gp.wait()
    wait_recv(gp_send.at[pl.ds(0, p_count - 1)], 4)
    for h in range(2):
        part = slice(h * half, (h + 1) * half)
        acc = gp_recv[0, :, part].astype(F32)
        for k in range(1, PLANE):
            acc += gp_recv[k, :, part].astype(F32)
        g_ref[1, :, part] = acc
    own_gq.wait()
    wait_recv(gq_send.at[pl.ds(0, Z - 1)], 5)
    for h in range(2):
        part = slice(h * half, (h + 1) * half)
        acc = gq_recv[0, :, part].astype(F32)
        for k in range(1, Z):
            acc += gq_recv[k, :, part].astype(F32)
        g_ref[0, :, part] = acc

    wait_send(qbuf.at[pl.ds(0, Z - 1)], 0)
    wait_send(pbuf.at[pl.ds(0, p_count - 1)], 1)
    wait_send(qbuf.at[pl.ds(0, Z)], 2)
    wait_send(statbuf.at[pl.ds(0, q_count - 1)], 3)
    wait_send(gp_send.at[pl.ds(0, p_count - 1)], 4)
    wait_send(gq_send.at[pl.ds(0, Z - 1)], 5)
    wait_send(lossbuf.at[pl.ds(0, PLANE - 1)], 6)


def hand_out(all_ref, loss_out, gq_out, gp_out, narrow, sem):
    narrow[...] = all_ref[:2].astype(BF16)
    copies = (pltpu.make_async_copy(all_ref.at[2, pl.ds(0, 1), pl.ds(0, LANES)], loss_out, sem.at[2]),
              pltpu.make_async_copy(narrow.at[0], gq_out, sem.at[0]), pltpu.make_async_copy(narrow.at[1], gp_out, sem.at[1]))
    for copy in copies:
        copy.start()
    for copy in copies:
        copy.wait()


def per_device(queries, passages, positive):
    own, width = queries.shape
    n_q, n_p = Z * CORES, PLANE
    vmem, hbm = pl.BlockSpec(memory_space=pltpu.VMEM), pl.BlockSpec(memory_space=pltpu.HBM)
    out = pl.pallas_call(
        functools.partial(kernel, n_q * own * PLANE),
        out_shape=jax.ShapeDtypeStruct((3, own, width), F32),
        in_specs=[hbm, hbm, hbm],
        out_specs=vmem,
        scratch_shapes=[
            pltpu.SMEM((own,), jnp.int32),
            pltpu.VMEM((own, width + LANES), BF16),
            pltpu.VMEM((own, width), BF16),
            pltpu.VMEM((n_q, own, width + LANES), BF16),
            pltpu.VMEM((n_p, own, width), BF16),
            pltpu.VMEM((n_q * own, width + LANES), F32),
            pltpu.VMEM((n_p * own, width), F32),
            pltpu.VMEM((n_q, 1, 3 * LANES), F32),
            pltpu.VMEM((1, 3 * LANES), F32),
            pltpu.VMEM((n_p, own, width), BF16),
            pltpu.VMEM((PLANE, own, width), BF16),
            pltpu.VMEM((n_p, own, width), BF16),
            pltpu.VMEM((n_p * own, n_q * own), F32),
            pltpu.VMEM((n_p * own, n_q * own), F32),
            pltpu.VMEM((Z, own, width), BF16),
            pltpu.VMEM((Z, own, width), BF16),
            pltpu.VMEM((PLANE, 1, LANES), F32),
            pltpu.VMEM((1, LANES), F32),
            pltpu.SemaphoreType.DMA((7,)),
            pltpu.SemaphoreType.DMA((9,)),
            pltpu.SemaphoreType.DMA((9,)),
            pltpu.SemaphoreType.DMA((Z,)),
        ],
        compiler_params=pltpu.CompilerParams(
            collective_id=0, has_side_effects=True, vmem_limit_bytes=32 * 1024 * 1024),
    )(*(pltpu.with_memory_space_constraint(a, pltpu.HBM) for a in (queries, passages, positive)))
    loss, gq, gp = pl.pallas_call(
        hand_out,
        out_shape=(
            jax.ShapeDtypeStruct((1, LANES), F32),
            jax.ShapeDtypeStruct((own, width), BF16),
            jax.ShapeDtypeStruct((own, width), BF16),
        ),
        in_specs=[vmem],
        out_specs=(hbm, hbm, hbm),
        scratch_shapes=[pltpu.VMEM((2, own, width), BF16), pltpu.SemaphoreType.DMA((3,))],
    )(pltpu.with_memory_space_constraint(out, pltpu.VMEM))
    return loss[0, 0], gq, gp


def solution(mesh):
    placed = (P(("row", "col"), None), P(("row", "col"), None), P(("row", "col")))
    return jax.shard_map(
        per_device,
        mesh=mesh,
        in_specs=placed,
        out_specs=(P(), P(("row", "col"), None), P(("row", "col"), None)),
        check_vma=False,
    )
```

```python
import functools

import jax
import jax.numpy as jnp
from jax import lax
from jax.experimental import pallas as pl
from jax.experimental.pallas import tpu as pltpu
from jax.sharding import PartitionSpec as P

MESH = pl.DeviceIdType.MESH
X, Y, Z, CORES = 4, 4, 8, 2
PLANE = X * Y
LANES = 128
F32, BF16 = jnp.float32, jnp.bfloat16


def ring(step, n):
    return min(step, n - step)


PLANE_STEPS = sorted(
    ((dx, dy) for dx in range(X) for dy in range(Y) if dx or dy),
    key=lambda s: -(ring(s[0], X) + ring(s[1], Y)))
LINE_STEPS = sorted(range(1, Z), key=lambda s: -ring(s, Z))


def kernel(total, q_hbm, p_hbm, pos_hbm, g_ref,
           pos, stage, p_own, qbuf, pbuf, qwide, pwide, statbuf, stat_own,
           gp_send, gp_recv, p_other, score_own, score_other, gq_send, gq_recv, lossbuf, loss_own,
           local_sem, send_sem, recv_sem, land_sem):
    row, col = lax.axis_index("row"), lax.axis_index("col")
    x, z, core = row >> 1, col >> 2, col & 1
    y = (col & 2) + (row & 1)
    chip = x * Y + y
    own, width = q_hbm.shape
    half = width // 2
    q_slot = core * Z + z
    other = (row, col ^ 1)
    xs, ys = [(x + d) & (X - 1) for d in range(X)], [(y + d) & (Y - 1) for d in range(Y)]
    x_row, y_row = [px * 2 for px in xs], [py & 1 for py in ys]
    y_col = [z * 4 + (py & 2) for py in ys]
    x_slot = [px * Y for px in xs]
    zs = [(z + d) & (Z - 1) for d in range(Z)]
    z_col = [pz * 4 + (col & 2) for pz in zs]

    def on_plane(step):
        dx, dy = step
        return (x_row[dx] + y_row[dy], y_col[dy] + core)

    def on_line(step, c):
        return (row, z_col[step] + c)

    loads = [
        pltpu.make_async_copy(pos_hbm, pos, local_sem.at[0]),
        pltpu.make_async_copy(p_hbm, p_own, local_sem.at[1]),
        pltpu.make_async_copy(q_hbm, stage.at[:, pl.ds(0, width)], local_sem.at[2]),
    ]
    for load in loads:
        load.start()
    barrier = pltpu.get_barrier_semaphore()

    def greet(device):
        pl.semaphore_signal(barrier, inc=1, device_id=device, device_id_type=MESH)

    for far in range(X // 2 + Y // 2, 0, -1):
        for step in PLANE_STEPS:
            if ring(step[0], X) + ring(step[1], Y) == far:
                greet(on_plane(step))
        for step in LINE_STEPS:
            if ring(step, Z) == far:
                for c in range(CORES):
                    greet(on_line(step, c))
    greet(other)

    loads[0].wait()
    lane = lax.broadcasted_iota(jnp.int32, (1, LANES), 1)
    codes = []
    for k in range(own):
        index = pos[k]
        codes.append(((lane == index // 32) | (lane == 32 + index % 32)).astype(F32))
    code = jnp.concatenate(codes, axis=0).astype(BF16)
    for load in loads[1:]:
        load.wait()
    stage[:, width:] = code

    pl.semaphore_wait(barrier, PLANE - 1 + (Z - 1) * CORES + 1)

    def send(src, dst, to, kind, landed=None):
        return pltpu.make_async_remote_copy(
            src_ref=src, dst_ref=dst, send_sem=send_sem.at[kind],
            recv_sem=recv_sem.at[kind] if landed is None else landed,
            device_id=to, device_id_type=MESH)

    for step in LINE_STEPS:
        send(stage, qbuf.at[q_slot], on_line(step, core), 0, land_sem.at[step]).start()
    for step in PLANE_STEPS:
        send(p_own, pbuf.at[chip], on_plane(step), 1).start()
    send(stage, qbuf.at[q_slot], other, 2).start()
    own_q = pltpu.make_async_copy(stage, qbuf.at[q_slot], local_sem.at[3])
    own_p = pltpu.make_async_copy(p_own, pbuf.at[chip], local_sem.at[4])
    own_q.start()
    own_p.start()

    def wait_recv(ref, kind):
        pltpu.make_async_copy(ref, ref, recv_sem.at[kind]).wait()

    def wait_send(ref, kind):
        pltpu.make_async_copy(ref, ref, send_sem.at[kind]).wait()

    p_count, q_count = PLANE, Z * CORES
    n_p, n_q = p_count * own, q_count * own
    slot = lax.broadcasted_iota(jnp.int32, (n_p, LANES), 0)
    p_chip = slot // own
    p_row = p_chip // Y * 2 + p_chip % 2
    p_lane = lax.broadcasted_iota(jnp.int32, (n_p, LANES), 1)

    def passage_code(c):
        p_id = (p_row * 32 + z * 4 + p_chip % Y // 2 * 2 + c) * own + slot % own
        return ((p_lane == p_id // 32) | (p_lane == 32 + p_id % 32)).astype(F32).astype(BF16)

    for step in LINE_STEPS[::-1]:
        landed = qbuf.at[core * Z + zs[Z - step]]
        pltpu.make_async_copy(landed, landed, land_sem.at[step]).wait()
        send(landed, landed, other, 2).start()
    own_p.wait()
    own_q.wait()
    wait_recv(pbuf.at[pl.ds(0, p_count - 1)], 1)
    give_passages = send(pbuf, p_other, other, 7)
    give_passages.start()
    for s in range(p_count):
        pwide[s * own:(s + 1) * own, :] = pbuf[s].astype(F32)
    passages = pwide[...].astype(BF16)
    wait_recv(qbuf.at[pl.ds(0, Z)], 2)
    for s in range(q_count):
        qwide[s * own:(s + 1) * own, :] = qbuf[s].astype(F32)
    queries = qwide[:, :width].astype(BF16)
    q_code = qwide[:, width:].astype(BF16)

    contract_last = (((1,), (1,)), ((), ()))
    scores = lax.dot_general(passages, queries, contract_last, preferred_element_type=F32)

    def match(c):
        return lax.dot_general(passage_code(c), q_code, contract_last, preferred_element_type=F32) > 1.5

    matched = match(core)

    peak = jnp.max(scores, axis=0, keepdims=True)
    stat_own[:, :n_q] = peak
    stat_own[:, LANES:LANES + n_q] = jnp.sum(jnp.exp(scores - peak), axis=0, keepdims=True)
    stat_own[:, 2 * LANES:2 * LANES + n_q] = jnp.sum(jnp.where(matched, scores, 0.0), axis=0, keepdims=True)
    statbuf[pl.ds(q_slot, 1)] = stat_own[...][None]
    for step in LINE_STEPS:
        for c in range(CORES):
            send(stat_own, statbuf.at[q_slot], on_line(step, c), 3).start()
    send(stat_own, statbuf.at[q_slot], other, 3).start()
    score_own[...] = scores
    give_scores = send(score_own, score_other, other, 8)
    give_scores.start()
    matched_other = match(1 - core)
    give_passages.wait()
    for s in range(p_count):
        pwide[s * own:(s + 1) * own, :] = p_other[s].astype(F32)
    passages_other = pwide[...].astype(BF16)
    give_scores.wait()
    wait_recv(statbuf.at[pl.ds(0, q_count - 1)], 3)
    stats = statbuf[...]
    peaks, sums, picks = stats[:, :, :n_q], stats[:, :, LANES:LANES + n_q], stats[:, :, 2 * LANES:2 * LANES + n_q]
    row_peak = jnp.max(peaks, axis=0)
    totals = jnp.sum(sums * jnp.exp(peaks - row_peak[None]), axis=0)
    positive_score = jnp.sum(picks, axis=0)

    def weigh(block, match):
        return jnp.exp(block - row_peak) / totals - match.astype(F32)

    wide = weigh(scores, matched)
    weights = wide.astype(BF16)

    loss_own[...] = jnp.zeros_like(loss_own)
    loss_own[:, :n_q] = row_peak + jnp.log(totals) - positive_score
    lossbuf[pl.ds(chip, 1)] = loss_own[...][None]
    for step in PLANE_STEPS:
        send(loss_own, lossbuf.at[chip], on_plane(step), 6).start()
    for at in range(0, width, 512):
        part = jnp.dot(weights, queries[:, at:at + 512], preferred_element_type=F32).astype(BF16)
        for s in range(p_count):
            gp_send[s, :, at:at + 512] = part[s * own:(s + 1) * own]
    for step in PLANE_STEPS:
        send(gp_send.at[x_slot[step[0]] + ys[step[1]]], gp_recv.at[chip], on_plane(step), 4).start()
    own_gp = pltpu.make_async_copy(gp_send.at[chip], gp_recv.at[chip], local_sem.at[5])
    own_gp.start()

    def of_mine(w):
        return jnp.where(core == 0, w[:, :n_q // 2], w[:, n_q // 2:]).astype(BF16)

    w_mine = jnp.concatenate([of_mine(wide), of_mine(weigh(score_other[...], matched_other))], axis=0)
    all_passages = jnp.concatenate([passages, passages_other], axis=0)

    for at in range(0, width, 512):
        part = lax.dot_general(w_mine, all_passages[:, at:at + 512], (((0,), (0,)), ((), ())),
                               preferred_element_type=F32).astype(BF16)
        for s in range(Z):
            gq_send[s, :, at:at + 512] = part[s * own:(s + 1) * own]
    for step in LINE_STEPS:
        send(gq_send.at[zs[step]], gq_recv.at[z], on_line(step, core), 5).start()
    own_gq = pltpu.make_async_copy(gq_send.at[z], gq_recv.at[z], local_sem.at[6])
    own_gq.start()

    wait_recv(lossbuf.at[pl.ds(0, PLANE - 1)], 6)
    loss = jnp.sum(jnp.sum(lossbuf[...], axis=0)) / total
    g_ref[2, :, :LANES] = jnp.broadcast_to(loss, (own, LANES))
    own_gp.wait()
    wait_recv(gp_send.at[pl.ds(0, p_count - 1)], 4)
    for h in range(2):
        part = slice(h * half, (h + 1) * half)
        acc = gp_recv[0, :, part].astype(F32)
        for k in range(1, PLANE):
            acc += gp_recv[k, :, part].astype(F32)
        g_ref[1, :, part] = acc
    own_gq.wait()
    wait_recv(gq_send.at[pl.ds(0, Z - 1)], 5)
    for h in range(2):
        part = slice(h * half, (h + 1) * half)
        acc = gq_recv[0, :, part].astype(F32)
        for k in range(1, Z):
            acc += gq_recv[k, :, part].astype(F32)
        g_ref[0, :, part] = acc

    wait_send(qbuf.at[pl.ds(0, Z - 1)], 0)
    wait_send(pbuf.at[pl.ds(0, p_count - 1)], 1)
    wait_send(qbuf.at[pl.ds(0, Z)], 2)
    wait_send(statbuf.at[pl.ds(0, q_count - 1)], 3)
    wait_send(gp_send.at[pl.ds(0, p_count - 1)], 4)
    wait_send(gq_send.at[pl.ds(0, Z - 1)], 5)
    wait_send(lossbuf.at[pl.ds(0, PLANE - 1)], 6)


def hand_out(all_ref, loss_out, gq_out, gp_out, narrow, sem):
    narrow[...] = all_ref[:2].astype(BF16)
    copies = (pltpu.make_async_copy(all_ref.at[2, pl.ds(0, 1), pl.ds(0, LANES)], loss_out, sem.at[2]),
              pltpu.make_async_copy(narrow.at[0], gq_out, sem.at[0]), pltpu.make_async_copy(narrow.at[1], gp_out, sem.at[1]))
    for copy in copies:
        copy.start()
    for copy in copies:
        copy.wait()


def per_device(queries, passages, positive):
    own, width = queries.shape
    n_q, n_p = Z * CORES, PLANE
    vmem, hbm = pl.BlockSpec(memory_space=pltpu.VMEM), pl.BlockSpec(memory_space=pltpu.HBM)
    out = pl.pallas_call(
        functools.partial(kernel, n_q * own * PLANE),
        out_shape=jax.ShapeDtypeStruct((3, own, width), F32),
        in_specs=[hbm, hbm, hbm],
        out_specs=vmem,
        scratch_shapes=[
            pltpu.SMEM((own,), jnp.int32),
            pltpu.VMEM((own, width + LANES), BF16),
            pltpu.VMEM((own, width), BF16),
            pltpu.VMEM((n_q, own, width + LANES), BF16),
            pltpu.VMEM((n_p, own, width), BF16),
            pltpu.VMEM((n_q * own, width + LANES), F32),
            pltpu.VMEM((n_p * own, width), F32),
            pltpu.VMEM((n_q, 1, 3 * LANES), F32),
            pltpu.VMEM((1, 3 * LANES), F32),
            pltpu.VMEM((n_p, own, width), BF16),
            pltpu.VMEM((PLANE, own, width), BF16),
            pltpu.VMEM((n_p, own, width), BF16),
            pltpu.VMEM((n_p * own, n_q * own), F32),
            pltpu.VMEM((n_p * own, n_q * own), F32),
            pltpu.VMEM((Z, own, width), BF16),
            pltpu.VMEM((Z, own, width), BF16),
            pltpu.VMEM((PLANE, 1, LANES), F32),
            pltpu.VMEM((1, LANES), F32),
            pltpu.SemaphoreType.DMA((7,)),
            pltpu.SemaphoreType.DMA((9,)),
            pltpu.SemaphoreType.DMA((9,)),
            pltpu.SemaphoreType.DMA((Z,)),
        ],
        compiler_params=pltpu.CompilerParams(
            collective_id=0, has_side_effects=True, vmem_limit_bytes=32 * 1024 * 1024),
    )(*(pltpu.with_memory_space_constraint(a, pltpu.HBM) for a in (queries, passages, positive)))
    loss, gq, gp = pl.pallas_call(
        hand_out,
        out_shape=(
            jax.ShapeDtypeStruct((1, LANES), F32),
            jax.ShapeDtypeStruct((own, width), BF16),
            jax.ShapeDtypeStruct((own, width), BF16),
        ),
        in_specs=[vmem],
        out_specs=(hbm, hbm, hbm),
        scratch_shapes=[pltpu.VMEM((2, own, width), BF16), pltpu.SemaphoreType.DMA((3,))],
    )(pltpu.with_memory_space_constraint(out, pltpu.VMEM))
    return loss[0, 0], gq, gp


def solution(mesh):
    placed = (P(("row", "col"), None), P(("row", "col"), None), P(("row", "col")))
    return jax.shard_map(
        per_device,
        mesh=mesh,
        in_specs=placed,
        out_specs=(P(), P(("row", "col"), None), P(("row", "col"), None)),
        check_vma=False,
    )
```
